512 devices in a mesh: row: 16 (over x, y_hi), col: 16 (over z, core), layer: 2 (over y_lo).
Axes of the slice: x: 4, y: 8 (y_hi: 4, y_lo: 2; y = y_hi * 2 + y_lo), z: 8, core: 2. Of those that a mesh axis runs over, the one named last changes fastest.
Arguments:
- a_blocks: bfloat16 [16, 16, 2, 16, 2, 128, 128], P('row', 'col', 'layer'), may hold values from -6 to 6
- a_cols: int32 [16, 16, 2, 16, 2], P('row', 'col', 'layer'), may hold values from 0 to 47, as said below
- a_count: int32 [16, 16, 2, 16], P('row', 'col', 'layer'), may hold values from 1 to 2
- b_blocks: bfloat16 [16, 16, 2, 48, 2, 128, 128], P('row', 'col', 'layer'), may hold values from -0.5 to 0.5
- b_cols: int32 [16, 16, 2, 48, 2], P('row', 'col', 'layer'), may hold values from 0 to 47, as said below
- b_count: int32 [16, 16, 2, 48], P('row', 'col', 'layer'), may hold values from 1 to 2
- c_cols: int32 [16, 16, 16, 2], P('row', 'col'), may hold values from 0 to 47, as said below
Outputs:
- c_blocks: bfloat16 [16, 16, 16, 2, 128, 128], P('row', 'col', 'layer')
The draws below stay inside these ranges and needn't reach their ends.
Inputs may be any that keep to these rules, and one draw needn't show every extreme that they name: a_cols of block row r is one of 3 * r - 1, 3 * r, 3 * r + 1 modulo 48; the slots of one block row are distinct. b_cols of block row m is one of m - 1, m, m + 1 modulo 48; the slots of one block row are distinct. c_cols of block row r is one of 3 * r - 1, 3 * r, 3 * r + 1 modulo 48; the slots of one block row are distinct.
All inputs are finite; a program needn't handle non-finite values.
Results may differ from the reference program's by a relative error of at most 0.001.
Values may be sent and summed in bfloat16 or wider, within the bound.
No kernel may reach another device: no remote copies, remote signals or barrier semaphores. Data moves between devices by JAX's collectives and lax.ppermute only.
A program may use at most 64 MiB of HBM per device.

```python
import jax
import jax.numpy as jnp
from jax import lax

BS = 128
PB = 48
PR = 16
KA = 2
KB = 2
KC = 2
STEPS = 2
STRIDE = 3
N_ROW = 16
N_COL = 16
N_LAYER = 2


def band_offsets(key, extent):
    last = len(extent) - 1
    first_offset = jax.random.randint(jax.random.fold_in(key, 1), extent[:-1] + (1,), 0, 3)
    offset_step = jax.random.randint(jax.random.fold_in(key, 2), extent[:-1] + (1,), 1, 3)
    slot_index = lax.broadcasted_iota(jnp.int32, extent, last)
    return (first_offset + slot_index * offset_step) % 3 - 1


def draw_a_cols(key, part):
    key = jax.random.fold_in(key, 11)
    extent = (N_ROW, N_COL, N_LAYER, PR, KA)
    centre = lax.broadcasted_iota(jnp.int32, extent, 3) * STRIDE
    return ((centre + band_offsets(key, extent)) % PB).astype(jnp.int32)


def draw_b_cols(key, part):
    key = jax.random.fold_in(key, 23)
    extent = (N_ROW, N_COL, N_LAYER, PB, KB)
    centre = lax.broadcasted_iota(jnp.int32, extent, 3)
    return ((centre + band_offsets(key, extent)) % PB).astype(jnp.int32)


def draw_c_cols(key, part):
    key = jax.random.fold_in(key, 37)
    extent = (N_ROW, N_COL, PR, KC)
    centre = lax.broadcasted_iota(jnp.int32, extent, 2) * STRIDE
    return ((centre + band_offsets(key, extent)) % PB).astype(jnp.int32)


def plant(result, key, least, high):
    dims = result.shape
    spot = [jax.random.randint(jax.random.fold_in(key, axis), (), 0, dims[axis]) for axis in range(len(dims))]
    result = result.at[tuple(spot)].set(least)
    longest = dims.index(max(dims))
    spot[longest] = (spot[longest] + 1) % dims[longest]
    return result.at[tuple(spot)].set(high)


def block_scale(own_key, shape, pieces, smallest, largest):
    def one(dim, parts):
        steps = jax.random.uniform(jax.random.fold_in(jax.random.fold_in(own_key, 6), dim), (parts,), jnp.float32, smallest / len(pieces), largest / len(pieces))
        return jnp.repeat(jnp.exp(steps), shape[dim] // parts).reshape((-1,) + (1,) * (len(shape) - dim - 1))

    level = one(*pieces[0])
    for cut in pieces[1:]:
        level = level * one(*cut)
    return level


def noise(own_key, shape, width, limit, shards=(), kind=jnp.bfloat16):
    level = block_scale(own_key, shape, shards, -0.22, 0.18) if shards else 1.0
    values = jax.random.normal(own_key, shape, jnp.float32) * width * level
    return jnp.minimum(jnp.maximum(values, -limit), limit).astype(kind)


def setup_inputs(seed: int = 0) -> dict:
    splits = jax.random.split(jax.random.key(seed), 8)
    a_blocks = noise(splits[0], (N_ROW, N_COL, N_LAYER, PR, KA, BS, BS), 1.0, 6.0, ((0, 16), (1, 16), (2, 2)))
    a_cols = draw_a_cols(jax.random.fold_in(splits[7], 71), 0)
    a_count = plant(jax.random.randint(splits[2], (N_ROW, N_COL, N_LAYER, PR), 1, KA + 1), jax.random.fold_in(splits[2], 1), 1, KA).astype(jnp.int32)
    b_blocks = noise(splits[3], (N_ROW, N_COL, N_LAYER, PB, KB, BS, BS), BS ** -0.5, 0.5, ((0, 16), (1, 16), (2, 2)))
    b_cols = draw_b_cols(jax.random.fold_in(splits[7], 71), 0)
    b_count = plant(jax.random.randint(splits[5], (N_ROW, N_COL, N_LAYER, PB), 1, KB + 1), jax.random.fold_in(splits[5], 1), 1, KB).astype(jnp.int32)
    c_cols = draw_c_cols(jax.random.fold_in(splits[7], 71), 0)
    return dict(a_blocks=a_blocks, a_cols=a_cols, a_count=a_count, b_blocks=b_blocks, b_cols=b_cols, b_count=b_count, c_cols=c_cols)


def panel_product(a_panel, a_index, a_live, b_panel, b_index, b_live, out_cols):
    chosen = jnp.take(b_panel, a_index, axis=0).astype(jnp.float32)
    chosen_cols = jnp.take(b_index, a_index, axis=0)
    chosen_live = jnp.take(b_live, a_index, axis=0)
    slot_a = lax.broadcasted_iota(jnp.int32, chosen_cols.shape, 1)
    slot_b = lax.broadcasted_iota(jnp.int32, chosen_cols.shape, 2)
    usable = (slot_a < a_live[:, None, None]) & (slot_b < chosen_live[:, :, None])
    matches = (chosen_cols[:, :, :, None] == out_cols[:, None, None, :]) & usable[:, :, :, None]
    products = jnp.einsum("rtxy,rtuyz->rtuxz", a_panel.astype(jnp.float32), chosen,
                          precision=lax.Precision.HIGHEST)
    return jnp.einsum("rtuv,rtuxz->rvxz", matches.astype(jnp.float32), products,
                      precision=lax.Precision.HIGHEST)


def reference(a_blocks, a_cols, a_count, b_blocks, b_cols, b_count, c_cols):
    def row_terms(row_index):
        a_row = a_blocks[row_index]
        a_row_cols = a_cols[row_index]
        a_row_live = a_count[row_index]
        out_row = c_cols[row_index]
        accumulated = jnp.zeros((N_COL, PR, KC, BS, BS), jnp.float32)
        for cannon_step in range(STEPS):
            source = (row_index + cannon_step) % N_ROW
            b_row = b_blocks[source]
            b_row_cols = b_cols[source]
            b_row_live = b_count[source]
            for layer_index in range(N_LAYER):
                a_panels = jnp.roll(a_row[:, layer_index], -cannon_step, axis=0)
                a_lists = jnp.roll(a_row_cols[:, layer_index], -cannon_step, axis=0)
                a_lives = jnp.roll(a_row_live[:, layer_index], -cannon_step, axis=0)
                accumulated = accumulated + jax.vmap(panel_product)(
                    a_panels, a_lists, a_lives,
                    b_row[:, layer_index], b_row_cols[:, layer_index], b_row_live[:, layer_index],
                    out_row)
        return accumulated.astype(jnp.bfloat16)

    return lax.map(row_terms, jnp.arange(N_ROW, dtype=jnp.int32))
```

```python
import functools

import jax
import jax.numpy as jnp
from jax import lax
from jax.experimental import pallas as pl
from jax.experimental.pallas import tpu as pltpu
from jax.sharding import PartitionSpec as P

BS = 128
TOP = 32700.0
STEP = 0.08664339756999316
LEAST = 1e-33
TAIL = 16
VMEM_LIMIT = 40 * 1024 * 1024


def row_product(a_ref, a_row, b_ref, r, a_cols, a_count, b_cols, b_count, c_cols):
    slots_a, slots_b, slots_c = a_ref.shape[1], b_ref.shape[1], c_cols.shape[1]
    left, right = [], []
    for t in range(slots_a):
        m = a_cols[r, t]
        live = t < a_count[r]
        wide = []
        for v in range(slots_c):
            wanted = c_cols[r, v]
            slot = jnp.int32(0)
            found = jnp.int32(0)
            for u in range(slots_b):
                hit = live & (u < b_count[m]) & (b_cols[m, u] == wanted)
                slot = jnp.where(hit, jnp.int32(u), slot)
                found = jnp.where(hit, jnp.int32(1), found)
            block = b_ref[m, slot]
            wide.append(jnp.where(found == 1, block, jnp.zeros_like(block)))
        left.append(a_ref[a_row, t])
        right.append(jnp.concatenate(wide, axis=1))
    return jnp.dot(
        jnp.concatenate(left, axis=1),
        jnp.concatenate(right, axis=0),
        preferred_element_type=jnp.float32,
    )


def encode(value):
    peak = jnp.maximum(jnp.max(jnp.abs(value), axis=0, keepdims=True), LEAST)
    number = jnp.ceil(jnp.log(peak) * (1.0 / STEP))
    code = jnp.round(value * (TOP * jnp.exp(number * -STEP)))
    code = jnp.clip(code, -32767.0, 32767.0)
    return code.astype(jnp.int32).astype(jnp.int16), number.astype(jnp.int32)


def decode(code, number):
    scale = jnp.exp(number.astype(jnp.float32) * STEP) * (1.0 / TOP)
    return code.astype(jnp.int32).astype(jnp.float32) * scale


def store_payload(out_ref, products):
    numbers = []
    for k, value in enumerate(products):
        code, number = encode(value)
        out_ref[pl.ds(k * BS, BS), :] = code
        numbers.append(number)
    numbers += [jnp.zeros_like(numbers[0])] * (TAIL - len(numbers))
    tail = jnp.concatenate(numbers, axis=0)
    out_ref[pl.ds(len(products) * BS, TAIL), :] = tail.astype(jnp.int16)


def local_kernel(half, a_cols, a_count, b_cols, b_count, c_cols, a_ref, b_ref, own_ref, out_ref):
    rows = a_ref.shape[0] // 2
    lists = (a_cols, a_count, b_cols, b_count, c_cols)
    other = (1 - half[0]) * rows
    store_payload(
        out_ref, [row_product(a_ref, other + k, b_ref, other + k, *lists) for k in range(rows)]
    )
    own = half[0] * rows
    for k in range(rows):
        own_ref[pl.ds(k * BS, BS), :] = row_product(a_ref, own + k, b_ref, own + k, *lists)


def remote_kernel(first, a_cols, a_count, b_cols, b_count, c_cols, a_ref, b_ref, out_ref):
    lists = (a_cols, a_count, b_cols, b_count, c_cols)
    rows = a_ref.shape[0]
    store_payload(
        out_ref, [row_product(a_ref, k, b_ref, first[0] + k, *lists) for k in range(rows)]
    )


def add_payload(total, ref, k, rows):
    tail = ref[pl.ds(rows * BS, TAIL), :].astype(jnp.int32)
    return total + decode(ref[pl.ds(k * BS, BS), :], tail[k : k + 1, :])


def first_sum_kernel(own_ref, cross_ref, out_ref):
    rows = own_ref.shape[0] // BS
    for k in range(rows):
        out_ref[pl.ds(k * BS, BS), :] = add_payload(own_ref[pl.ds(k * BS, BS), :], cross_ref, k, rows)


def last_sum_kernel(half, sum_ref, layer_low, layer_high, same_ref, out_ref):
    rows, slots = out_ref.shape[0], out_ref.shape[1]

    def finish(layer_ref):
        for k in range(rows):
            total = add_payload(sum_ref[pl.ds(k * BS, BS), :], layer_ref, k, rows)
            total = add_payload(total, same_ref, k, rows)
            for v in range(slots):
                out_ref[k, v] = total[:, v * BS : (v + 1) * BS].astype(out_ref.dtype)

    @pl.when(half[0] == 0)
    def _():
        finish(layer_low)

    @pl.when(half[0] == 1)
    def _():
        finish(layer_high)


SMEM = pl.BlockSpec(memory_space=pltpu.SMEM)
VMEM = pl.BlockSpec(memory_space=pltpu.VMEM)


def call(kernel, scalars, arrays, outs, flops, moved, name):
    return pl.pallas_call(
        kernel,
        in_specs=[SMEM] * len(scalars) + [VMEM] * len(arrays),
        out_specs=jax.tree.map(lambda _: VMEM, outs),
        out_shape=outs,
        compiler_params=pltpu.CompilerParams(vmem_limit_bytes=VMEM_LIMIT),
        cost_estimate=pl.CostEstimate(flops=flops, bytes_accessed=moved, transcendentals=0),
        name=name,
    )(*scalars, *arrays)


def local(mesh_shape, a_blocks, a_cols, a_count, b_blocks, b_cols, b_count, c_cols):
    n_row, n_col = mesh_shape["row"], mesh_shape["col"]
    a_panel, b_panel = a_blocks[0, 0, 0], b_blocks[0, 0, 0]
    a_index, a_live = a_cols[0, 0, 0], a_count[0, 0, 0]
    b_index, b_live = b_cols[0, 0, 0], b_count[0, 0, 0]
    out_cols = c_cols[0, 0]
    layer = lax.axis_index("layer").astype(jnp.int32)
    rows = a_panel.shape[0] // 2
    wide = out_cols.shape[1] * BS
    coded = jax.ShapeDtypeStruct((rows * BS + TAIL, wide), jnp.int16)
    summed = jax.ShapeDtypeStruct((rows * BS, wide), jnp.float32)
    result = jax.ShapeDtypeStruct((rows, out_cols.shape[1], BS, BS), jnp.bfloat16)

    def place(i, j, l):
        return ((i % n_row) * n_col + j % n_col) * 2 + l

    grid = [(i, j, l) for i in range(n_row) for j in range(n_col) for l in range(2)]

    def send(value, target, who=(0, 1)):
        pairs = [(place(i, j, l), place(*target(i, j, l))) for i, j, l in grid if l in who]
        return lax.ppermute(value, ("row", "col", "layer"), pairs)

    def to_user(i, j, l):
        return i + 1, j - 1, l

    half = layer[None]
    own_first = (layer * rows)[None]
    other_first = ((1 - layer) * rows)[None]

    a_other = send(lax.dynamic_slice_in_dim(a_panel, other_first[0], rows, 0), to_user)
    far_lists = send(jnp.concatenate([a_index, a_live[:, None]], axis=1), to_user)
    far_cols = send(out_cols, lambda i, j, l: (i + 1, j, l))
    a_own = send(lax.dynamic_slice_in_dim(a_panel, own_first[0], rows, 0), to_user)

    block_flops = 2 * BS * 2 * BS * wide
    own, other = call(
        local_kernel,
        (half, a_index, a_live, b_index, b_live, out_cols),
        (a_panel, b_panel),
        (summed, coded),
        2 * rows * block_flops,
        6 << 20,
        "step0",
    )
    low = send(other, lambda i, j, l: (i, j, 0), who=(1,))

    far_index, far_live = far_lists[:, :-1], far_lists[:, -1]
    lists = (far_index, far_live, b_index, b_live, far_cols)
    cross = call(
        remote_kernel, (other_first, *lists), (a_other, b_panel), coded, rows * block_flops, 5 << 20, "step1_cross"
    )
    cross_in = send(cross, lambda i, j, l: (i - 1, j, 1 - l))

    a_own, cross = lax.optimization_barrier((a_own, cross))
    same = call(
        remote_kernel, (own_first, *lists), (a_own, b_panel), coded, rows * block_flops, 5 << 20, "step1_same"
    )
    same_in = send(same, lambda i, j, l: (i - 1, j, l))
    high = send(lax.optimization_barrier((other, a_own))[0], lambda i, j, l: (i, j, 1), who=(0,))

    total = call(first_sum_kernel, (), (own, cross_in), summed, 1 << 20, 3 << 20, "sum_cross")
    total, same_in = lax.optimization_barrier((total, same_in))
    c = call(
        last_sum_kernel, (half,), (total, low, high, same_in), result, 1 << 20, 3 << 20, "sum_all"
    )
    return c[None, None]


def solution(mesh):
    return jax.shard_map(
        functools.partial(local, dict(mesh.shape)),
        mesh=mesh,
        in_specs=(
            P("row", "col", "layer", None, None, None, None),
            P("row", "col", "layer", None, None),
            P("row", "col", "layer", None),
            P("row", "col", "layer", None, None, None, None),
            P("row", "col", "layer", None, None),
            P("row", "col", "layer", None),
            P("row", "col", None, None),
        ),
        out_specs=P("row", "col", "layer", None, None, None),
        check_vma=False,
    )
```

```python
import functools

import jax
import jax.numpy as jnp
from jax import lax
from jax.experimental import pallas as pl
from jax.experimental.pallas import tpu as pltpu
from jax.sharding import PartitionSpec as P

BS = 128
TOP = 32700.0
STEP = 0.08664339756999316
LEAST = 1e-33
TAIL = 16
SLOTS_A, SLOTS_C = 2, 2
B_COLS, B_COUNT, A_COLS, A_COUNT, C_COLS = 0, 2, 3, 5, 6
VMEM_LIMIT = 16 * 1024 * 1024


def row_product(a_ref, a_row, b_ref, r, a_lists, b_lists, c_lists):
    left, right = [], []
    for t in range(SLOTS_A):
        m = a_lists[A_COLS + t, r]
        live = t < a_lists[A_COUNT, r]
        wide = []
        for v in range(SLOTS_C):
            wanted = c_lists[C_COLS + v, r]
            slot = jnp.int32(0)
            found = jnp.int32(0)
            for u in range(b_ref.shape[1]):
                hit = live & (u < b_lists[B_COUNT, m]) & (b_lists[B_COLS + u, m] == wanted)
                slot = jnp.where(hit, jnp.int32(u), slot)
                found = jnp.where(hit, jnp.int32(1), found)
            block = b_ref[m, slot]
            wide.append(jnp.where(found == 1, block, jnp.zeros_like(block)))
        left.append(a_ref[pl.ds((a_row * SLOTS_A + t) * BS, BS), :])
        right.append(jnp.concatenate(wide, axis=1))
    return jnp.dot(
        jnp.concatenate(left, axis=1),
        jnp.concatenate(right, axis=0),
        preferred_element_type=jnp.float32,
    )


def pack_lists(b_cols, b_count, a_cols, a_count, c_cols):
    lists = [b_cols.T, b_count[None], a_cols.T, a_count[None], c_cols.T]
    depth, wide = sum(x.shape[0] for x in lists), b_count.shape[0]
    pack, at = 0, 0
    for x in lists:
        height = x.shape[0]
        pack += lax.pad(x, jnp.int32(0), [(at, depth - at - height, 0), (0, wide - x.shape[1], 0)])
        at += height
    return pack


def encode(value):
    peak = jnp.maximum(jnp.max(jnp.abs(value), axis=0, keepdims=True), LEAST)
    number = jnp.ceil(jnp.log(peak) * (1.0 / STEP))
    code = jnp.round(value * (TOP * jnp.exp(number * -STEP)))
    code = jnp.clip(code, -32767.0, 32767.0)
    return code.astype(jnp.int32).astype(jnp.int16), number.astype(jnp.int32)


def decode(code, number):
    scale = jnp.exp(number.astype(jnp.float32) * STEP) * (1.0 / TOP)
    return code.astype(jnp.int32).astype(jnp.float32) * scale


def store_payload(out_ref, products):
    numbers = []
    for k, value in enumerate(products):
        code, number = encode(value)
        out_ref[pl.ds(k * BS, BS), :] = code
        numbers.append(number)
    numbers += [jnp.zeros_like(numbers[0])] * (TAIL - len(numbers))
    tail = jnp.concatenate(numbers, axis=0)
    out_ref[pl.ds(len(products) * BS, TAIL), :] = tail.astype(jnp.int16)


def head_kernel(first, pack_ref, a_hbm, out_ref, tile, sem):
    size = out_ref.shape[0] - TAIL
    start = pl.multiple_of(first[0] * SLOTS_A * BS, BS)
    copy = pltpu.make_async_copy(a_hbm.at[pl.ds(start, size)], out_ref.at[pl.ds(0, size)], sem)
    copy.start()
    tile[...] = jnp.zeros_like(tile)
    tile[pl.ds(0, pack_ref.shape[0]), pl.ds(0, pack_ref.shape[1])] = pack_ref[...].astype(jnp.float32)
    out_ref[pl.ds(size, TAIL), :] = tile[...].astype(out_ref.dtype)
    copy.wait()


def local_kernel(parts, half, pack, a_ref, b_ref, low_ref, high_ref, out_ref, *sent):
    rows = a_ref.shape[0] // (2 * SLOTS_A * BS)
    other = (1 - half[0]) * rows
    own = half[0] * rows
    for (same, start, _), ref in zip(parts, sent, strict=True):
        at = pl.multiple_of((jnp.where(same, own, other) + start) * SLOTS_A * BS, BS)
        ref[...] = a_ref[pl.ds(at, ref.shape[0]), :]
    store_payload(
        out_ref, [row_product(a_ref, other + k, b_ref, other + k, pack, pack, pack) for k in range(rows)]
    )
    for k in range(rows):
        ref, at = (low_ref, k) if k < rows // 2 else (high_ref, k - rows // 2)
        ref[pl.ds(at * BS, BS), :] = row_product(a_ref, own + k, b_ref, own + k, pack, pack, pack)


def remote_kernel(first, a_lists, b_lists, c_lists, a_ref, b_ref, out_ref):
    rows = a_ref.shape[0] // (SLOTS_A * BS)
    store_payload(
        out_ref,
        [row_product(a_ref, k, b_ref, first[0] + k, a_lists, b_lists, c_lists) for k in range(rows)],
    )


def payload_row(ref, k):
    rows = (ref.shape[0] - TAIL) // BS
    tail = ref[pl.ds(rows * BS, TAIL), :].astype(jnp.int32)
    return decode(ref[pl.ds(k * BS, BS), :], tail[k : k + 1, :])


def add_kernel(start, wanted, half, total_ref, layer_ref, part_ref, out_ref):
    rows = out_ref.shape[0] // BS
    for k in range(rows):
        out_ref[pl.ds(k * BS, BS), :] = total_ref[pl.ds(k * BS, BS), :] + payload_row(part_ref, k)

    @pl.when(half[0] == wanted)
    def _():
        for k in range(rows):
            out_ref[pl.ds(k * BS, BS), :] += payload_row(layer_ref, start + k)


def third_sum_kernel(half, low_ref, high_ref, layer_ref, part_ref, out_ref, rest_ref):
    rows = low_ref.shape[0] // BS
    slots = out_ref.shape[1]
    scale = jnp.where(half[0] == 1, 1.0, 0.0)
    for k in range(rows):
        total = low_ref[pl.ds(k * BS, BS), :] + payload_row(part_ref, k)
        total = total + jnp.where(half[0] == 1, payload_row(layer_ref, k), 0.0)
        for v in range(slots):
            out_ref[k, v] = total[:, v * BS : (v + 1) * BS].astype(out_ref.dtype)
        rest = jnp.where(half[0] == 1, payload_row(layer_ref, rows + k), 0.0)
        rest_ref[pl.ds(k * BS, BS), :] = high_ref[pl.ds(k * BS, BS), :] + rest


def last_sum_kernel(rest_ref, part_ref, _, out_ref):
    for k in range(out_ref.shape[0]):
        total = rest_ref[pl.ds(k * BS, BS), :] + payload_row(part_ref, k)
        for v in range(out_ref.shape[1]):
            out_ref[k, v] = total[:, v * BS : (v + 1) * BS].astype(out_ref.dtype)


SMEM = pl.BlockSpec(memory_space=pltpu.SMEM)
VMEM = pl.BlockSpec(memory_space=pltpu.VMEM)
HBM = pl.BlockSpec(memory_space=pltpu.HBM)


def call(kernel, scalars, arrays, outs, cost, name, out_specs=None, **more):
    return pl.pallas_call(
        kernel,
        in_specs=[SMEM] * len(scalars) + [VMEM] * len(arrays),
        out_specs=jax.tree.map(lambda _: VMEM, outs) if out_specs is None else out_specs,
        out_shape=outs,
        compiler_params=pltpu.CompilerParams(vmem_limit_bytes=VMEM_LIMIT),
        cost_estimate=pl.CostEstimate(flops=int(cost * US), bytes_accessed=0, transcendentals=0),
        name=name,
        **more,
    )(*scalars, *arrays)


PARTS = ((False, 0, 4), (False, 4, 4), (True, 0, 4), (True, 4, 4))
US = 1e9
COST_STEP0 = 2
COST_STEP1 = 10
COST_SUM = 10


def after(value, *others):
    return lax.optimization_barrier((value, *others))[0]


def local(mesh_shape, a_blocks, a_cols, a_count, b_blocks, b_cols, b_count, c_cols):
    n_row, n_col = mesh_shape["row"], mesh_shape["col"]
    a_panel, b_panel = a_blocks[0, 0, 0], b_blocks[0, 0, 0]
    a_index, a_live = a_cols[0, 0, 0], a_count[0, 0, 0]
    b_index, b_live = b_cols[0, 0, 0], b_count[0, 0, 0]
    out_cols = c_cols[0, 0]
    layer = lax.axis_index("layer").astype(jnp.int32)
    rows = a_panel.shape[0] // 2
    wide = out_cols.shape[1] * BS
    summed = jax.ShapeDtypeStruct((rows // 2 * BS, wide), jnp.float32)
    result = jax.ShapeDtypeStruct((rows, out_cols.shape[1], BS, BS), jnp.bfloat16)

    def coded(count):
        return jax.ShapeDtypeStruct((count * BS + TAIL, wide), jnp.int16)

    def place(i, j, l):
        return ((i % n_row) * n_col + j % n_col) * 2 + l

    grid = [(i, j, l) for i in range(n_row) for j in range(n_col) for l in range(2)]

    def send(name, value, target, who=(0, 1)):
        pairs = [(place(i, j, l), place(*target(i, j, l))) for i, j, l in grid if l in who]
        with jax.named_scope(name):
            return lax.ppermute(value, ("row", "col", "layer"), pairs)

    def to_user(i, j, l):
        return i + 1, j - 1, l

    half = layer[None]
    firsts = [jnp.where(same, layer, 1 - layer) * rows + start for same, start, _ in PARTS]

    pack = pack_lists(b_index, b_live, a_index, a_live, out_cols)
    row_size = SLOTS_A * BS
    a_panel = a_panel.reshape(-1, BS)
    head = pl.pallas_call(
        head_kernel,
        in_specs=[SMEM, VMEM, HBM],
        out_specs=VMEM,
        out_shape=jax.ShapeDtypeStruct((PARTS[0][2] * row_size + TAIL, BS), a_panel.dtype),
        scratch_shapes=[pltpu.VMEM((TAIL, BS), jnp.float32), pltpu.SemaphoreType.DMA],
        compiler_params=pltpu.CompilerParams(vmem_limit_bytes=VMEM_LIMIT),
        name="head",
    )(firsts[0][None], pack, a_panel)
    far_a = [send("send_a0", head, to_user)]

    parts = PARTS[1:]
    low, high, other, *a_parts = call(
        functools.partial(local_kernel, parts),
        (half, pack),
        (a_panel, b_panel),
        (
            summed,
            summed,
            coded(rows),
            *(jax.ShapeDtypeStruct((count * row_size, BS), a_panel.dtype) for _, _, count in parts),
        ),
        COST_STEP0,
        "step0",
    )
    down = send("send_layer_down", other, lambda i, j, l: (i, j, 0), who=(1,))
    far_cols = send("send_c_cols", after(pack, other), lambda i, j, l: (i + 1, j, l))
    far_a += [send(f"send_a{k + 1}", after(part, far_cols), to_user) for k, part in enumerate(a_parts[:-1])]

    far_lists = far_a[0][-TAIL:, : pack.shape[1]].astype(jnp.int32)
    back, before = [], []
    for k, ((same, _, count), first) in enumerate(zip(PARTS, firsts, strict=True)):
        product = call(
            remote_kernel,
            (first[None], far_lists, pack, far_cols),
            (after(far_a[k], *before), b_panel),
            coded(count),
            COST_STEP1,
            f"step1_part{k}",
        )
        before = [product]
        if k == 0:
            before.append(down)
            far_a.append(send(f"send_a{len(far_a)}", after(a_parts[-1], product), to_user))
        back.append(send(f"send_c{k}", product, lambda i, j, l, same=same: (i - 1, j, l if same else 1 - l)))
    up = send("send_layer_up", after(other, product), lambda i, j, l: (i, j, 1), who=(0,))

    add = functools.partial(call, outs=summed, cost=COST_SUM)
    low = add(functools.partial(add_kernel, 0, 0), (half,), (low, down, back[0]), name="sum_part0")
    high = add(functools.partial(add_kernel, rows // 2, 0), (half,), (after(high, low), down, back[1]), name="sum_part1")
    c, rest = call(third_sum_kernel, (half,), (low, high, up, back[2]), (result, summed), COST_SUM, "sum_part2")
    c = pl.pallas_call(
        last_sum_kernel,
        grid=(1,),
        in_specs=[pl.BlockSpec(summed.shape, lambda _: (0, 0)), pl.BlockSpec(coded(rows // 2).shape, lambda _: (0, 0)), pl.BlockSpec(memory_space=pl.ANY)],
        out_specs=pl.BlockSpec((rows // 2, *result.shape[1:]), lambda _: (1, 0, 0, 0)),
        out_shape=result,
        input_output_aliases={2: 0},
        compiler_params=pltpu.CompilerParams(vmem_limit_bytes=VMEM_LIMIT),
        name="sum_part3",
    )(rest, back[3], c)
    return c[None, None]


def solution(mesh):
    return jax.shard_map(
        functools.partial(local, dict(mesh.shape)),
        mesh=mesh,
        in_specs=(
            P("row", "col", "layer", None, None, None, None),
            P("row", "col", "layer", None, None),
            P("row", "col", "layer", None),
            P("row", "col", "layer", None, None, None, None),
            P("row", "col", "layer", None, None),
            P("row", "col", "layer", None),
            P("row", "col", None, None),
        ),
        out_specs=P("row", "col", "layer", None, None, None),
        check_vma=False,
    )
```

```python
import functools

import jax
import jax.numpy as jnp
from jax import lax
from jax.experimental import pallas as pl
from jax.experimental.pallas import tpu as pltpu
from jax.sharding import PartitionSpec as P

BS = 128
TOP = 32700.0
STEP = 0.08664339756999316
LEAST = 1e-33
TAIL = 16
SLOTS_A, SLOTS_C = 2, 2
B_COLS, B_COUNT, A_COLS, A_COUNT, C_COLS = 0, 2, 3, 5, 6
VMEM_LIMIT = 16 * 1024 * 1024


def row_product(a_ref, a_row, b_ref, r, a_lists, b_lists, c_lists):
    left, right = [], []
    for t in range(SLOTS_A):
        m = a_lists[A_COLS + t, r]
        live = t < a_lists[A_COUNT, r]
        wide = []
        for v in range(SLOTS_C):
            wanted = c_lists[C_COLS + v, r]
            slot = jnp.int32(0)
            found = jnp.int32(0)
            for u in range(b_ref.shape[1]):
                hit = live & (u < b_lists[B_COUNT, m]) & (b_lists[B_COLS + u, m] == wanted)
                slot = jnp.where(hit, jnp.int32(u), slot)
                found = jnp.where(hit, jnp.int32(1), found)
            block = b_ref[m, slot]
            wide.append(jnp.where(found == 1, block, jnp.zeros_like(block)))
        left.append(a_ref[pl.ds((a_row * SLOTS_A + t) * BS, BS), :])
        right.append(jnp.concatenate(wide, axis=1))
    return jnp.dot(
        jnp.concatenate(left, axis=1),
        jnp.concatenate(right, axis=0),
        preferred_element_type=jnp.float32,
    )


def pack_lists(b_cols, b_count, a_cols, a_count, c_cols):
    lists = [b_cols.T, b_count[None], a_cols.T, a_count[None], c_cols.T]
    depth, wide = sum(x.shape[0] for x in lists), b_count.shape[0]
    pack, at = 0, 0
    for x in lists:
        height = x.shape[0]
        pack += lax.pad(x, jnp.int32(0), [(at, depth - at - height, 0), (0, wide - x.shape[1], 0)])
        at += height
    return pack


def encode(value):
    peak = jnp.maximum(jnp.max(jnp.abs(value), axis=0, keepdims=True), LEAST)
    number = jnp.ceil(jnp.log(peak) * (1.0 / STEP))
    code = jnp.round(value * (TOP * jnp.exp(number * -STEP)))
    code = jnp.clip(code, -32767.0, 32767.0)
    return code.astype(jnp.int32).astype(jnp.int16), number.astype(jnp.int32)


def decode(code, number):
    scale = jnp.exp(number.astype(jnp.float32) * STEP) * (1.0 / TOP)
    return code.astype(jnp.int32).astype(jnp.float32) * scale


def store_payload(out_ref, products):
    numbers = []
    for k, value in enumerate(products):
        code, number = encode(value)
        for v in range(SLOTS_C):
            out_ref[pl.ds((k * SLOTS_C + v) * BS, BS), :] = code[:, v * BS : (v + 1) * BS]
            numbers.append(number[:, v * BS : (v + 1) * BS])
    size = len(numbers) * BS
    numbers += [jnp.zeros_like(numbers[0])] * (TAIL - len(numbers))
    out_ref[pl.ds(size, TAIL), :] = jnp.concatenate(numbers, axis=0).astype(jnp.int16)


def head_kernel(first, pack_ref, a_hbm, out_ref, tile, sem):
    size = out_ref.shape[0] - TAIL
    start = pl.multiple_of(first[0] * SLOTS_A * BS, BS)
    copy = pltpu.make_async_copy(a_hbm.at[pl.ds(start, size)], out_ref.at[pl.ds(0, size)], sem)
    copy.start()
    tile[...] = jnp.zeros_like(tile)
    tile[pl.ds(0, pack_ref.shape[0]), pl.ds(0, pack_ref.shape[1])] = pack_ref[...].astype(jnp.float32)
    out_ref[pl.ds(size, TAIL), :] = tile[...].astype(out_ref.dtype)
    copy.wait()


def local_kernel(parts, half, pack, a_ref, b_ref, own_ref, out_ref, *sent):
    rows = a_ref.shape[0] // (2 * SLOTS_A * BS)
    other = (1 - half[0]) * rows
    own = half[0] * rows
    for (same, start, _), ref in zip(parts, sent, strict=True):
        at = pl.multiple_of((jnp.where(same, own, other) + start) * SLOTS_A * BS, BS)
        ref[...] = a_ref[pl.ds(at, ref.shape[0]), :]
    store_payload(
        out_ref, [row_product(a_ref, other + k, b_ref, other + k, pack, pack, pack) for k in range(rows)]
    )
    for k in range(rows):
        own_ref[pl.ds(k * BS, BS), :] = row_product(a_ref, own + k, b_ref, own + k, pack, pack, pack)


def remote_kernel(first, a_lists, b_lists, c_lists, a_ref, b_ref, out_ref):
    rows = a_ref.shape[0] // (SLOTS_A * BS)
    store_payload(
        out_ref,
        [row_product(a_ref, k, b_ref, first[0] + k, a_lists, b_lists, c_lists) for k in range(rows)],
    )


def payload_row(ref, k):
    tail = ref[pl.ds(ref.shape[0] - TAIL, TAIL), :].astype(jnp.int32)
    blocks = range(k * SLOTS_C, (k + 1) * SLOTS_C)
    return jnp.concatenate([decode(ref[pl.ds(n * BS, BS), :], tail[n : n + 1, :]) for n in blocks], axis=1)


def add_kernel(part, half, total_ref, part_ref, *refs):
    *layer, out_ref = refs
    _, start, count = part
    for k in range(count):
        at = pl.ds((start + k) * BS, BS)
        out_ref[at, :] = total_ref[at, :] + payload_row(part_ref, k)
    for layer_ref in layer:

        @pl.when(half[0] == 0)
        def _():
            for k in range(out_ref.shape[0] // BS):
                out_ref[pl.ds(k * BS, BS), :] += payload_row(layer_ref, k)


def store_row(out_ref, k, total):
    for v in range(SLOTS_C):
        out_ref[k, v] = total[:, v * BS : (v + 1) * BS].astype(out_ref.dtype)


def early_sum_kernel(part, kept, half, total_ref, layer_ref, part_ref, out_ref, rest_ref):
    rows = out_ref.shape[0]
    _, start, count = part
    for k in range(rows):
        total = total_ref[pl.ds(k * BS, BS), :]
        if start <= k < start + count:
            total = total + payload_row(part_ref, k - start)
        total = total + jnp.where(half[0] == 1, payload_row(layer_ref, k), 0.0)
        if k < rows - kept:
            store_row(out_ref, k, total)
        else:
            rest_ref[pl.ds((k - rows + kept) * BS, BS), :] = total


def last_sum_kernel(rest_ref, part_ref, _, out_ref):
    for k in range(out_ref.shape[0]):
        store_row(out_ref, k, rest_ref[pl.ds(k * BS, BS), :] + payload_row(part_ref, k))


SMEM = pl.BlockSpec(memory_space=pltpu.SMEM)
VMEM = pl.BlockSpec(memory_space=pltpu.VMEM)
HBM = pl.BlockSpec(memory_space=pltpu.HBM)


def call(kernel, scalars, arrays, outs, cost, name, out_specs=None, **more):
    return pl.pallas_call(
        kernel,
        in_specs=[SMEM] * len(scalars) + [VMEM] * len(arrays),
        out_specs=jax.tree.map(lambda _: VMEM, outs) if out_specs is None else out_specs,
        out_shape=outs,
        compiler_params=pltpu.CompilerParams(vmem_limit_bytes=VMEM_LIMIT),
        cost_estimate=pl.CostEstimate(flops=int(cost * US), bytes_accessed=0, transcendentals=0),
        name=name,
        **more,
    )(*scalars, *arrays)


PARTS = ((False, 0, 4), (False, 4, 4), (True, 0, 4), (True, 4, 4))
US = 1e9
COST_STEP0 = 2
COST_STEP1 = 25
COST_FIRST = 6
COST_SUM = 1


def after(value, *others):
    return lax.optimization_barrier((value, *others))[0]


def local(mesh_shape, a_blocks, a_cols, a_count, b_blocks, b_cols, b_count, c_cols):
    n_row, n_col = mesh_shape["row"], mesh_shape["col"]
    a_panel, b_panel = a_blocks[0, 0, 0], b_blocks[0, 0, 0]
    a_index, a_live = a_cols[0, 0, 0], a_count[0, 0, 0]
    b_index, b_live = b_cols[0, 0, 0], b_count[0, 0, 0]
    out_cols = c_cols[0, 0]
    layer = lax.axis_index("layer").astype(jnp.int32)
    rows = a_panel.shape[0] // 2
    wide = out_cols.shape[1] * BS
    summed = jax.ShapeDtypeStruct((rows * BS, wide), jnp.float32)
    result = jax.ShapeDtypeStruct((rows, out_cols.shape[1], BS, BS), jnp.bfloat16)

    def coded(count):
        return jax.ShapeDtypeStruct((count * SLOTS_C * BS + TAIL, BS), jnp.int16)

    def place(i, j, l):
        return ((i % n_row) * n_col + j % n_col) * 2 + l

    grid = [(i, j, l) for i in range(n_row) for j in range(n_col) for l in range(2)]

    def send(name, value, target, who=(0, 1)):
        pairs = [(place(i, j, l), place(*target(i, j, l))) for i, j, l in grid if l in who]
        with jax.named_scope(name):
            return lax.ppermute(value, ("row", "col", "layer"), pairs)

    def to_user(i, j, l):
        return i + 1, j - 1, l

    half = layer[None]
    firsts = [jnp.where(same, layer, 1 - layer) * rows + start for same, start, _ in PARTS]

    pack = pack_lists(b_index, b_live, a_index, a_live, out_cols)
    row_size = SLOTS_A * BS
    a_panel = a_panel.reshape(-1, BS)
    head = pl.pallas_call(
        head_kernel,
        in_specs=[SMEM, VMEM, HBM],
        out_specs=VMEM,
        out_shape=jax.ShapeDtypeStruct((PARTS[0][2] * row_size + TAIL, BS), a_panel.dtype),
        scratch_shapes=[pltpu.VMEM((TAIL, BS), jnp.float32), pltpu.SemaphoreType.DMA],
        compiler_params=pltpu.CompilerParams(vmem_limit_bytes=VMEM_LIMIT),
        name="head",
    )(firsts[0][None], pack, a_panel)
    far_a = [send("send_a0", head, to_user)]

    parts = PARTS[1:]
    own, other, *a_parts = call(
        functools.partial(local_kernel, parts),
        (half, pack),
        (a_panel, b_panel),
        (
            summed,
            coded(rows),
            *(jax.ShapeDtypeStruct((count * row_size, BS), a_panel.dtype) for _, _, count in parts),
        ),
        COST_STEP0,
        "step0",
    )
    down = send("send_layer_down", other, lambda i, j, l: (i, j, 0), who=(1,))
    far_cols = send("send_c_cols", after(pack, other), lambda i, j, l: (i + 1, j, l))
    far_a.append(send("send_a1", a_parts[0], to_user))

    far_lists = far_a[0][-TAIL:, : pack.shape[1]].astype(jnp.int32)
    back, before = [], []
    for k, ((same, _, count), first) in enumerate(zip(PARTS, firsts, strict=True)):
        product = call(
            remote_kernel,
            (first[None], far_lists, pack, far_cols),
            (after(far_a[k], *before), b_panel),
            coded(count),
            COST_FIRST if k == 0 else COST_STEP1,
            f"step1_part{k}",
        )
        before = [product]
        if k == 0:
            before.append(down)
        if k + 1 < len(a_parts):
            far_a.append(send(f"send_a{k + 2}", after(a_parts[k + 1], product), to_user))
        if k == len(PARTS) - 3:
            up = send("send_layer_up", after(other, product), lambda i, j, l: (i, j, 1), who=(0,))
        back.append(send(f"send_c{k}", product, lambda i, j, l, same=same: (i - 1, j, l if same else 1 - l)))
    total, more = own, (down,)
    for k, part in enumerate(PARTS[:-2]):
        total = call(
            functools.partial(add_kernel, part),
            (half,),
            (total, back[k], *more),
            summed,
            COST_SUM,
            f"sum_part{k}",
            input_output_aliases={1: 0},
        )
        more = ()
    kept = PARTS[-1][2]
    rest = jax.ShapeDtypeStruct((kept * BS, wide), jnp.float32)
    c, rest = call(
        functools.partial(early_sum_kernel, PARTS[-2], kept), (half,), (total, up, back[-2]), (result, rest), COST_SUM, "sum_early"
    )
    c = pl.pallas_call(
        last_sum_kernel,
        grid=(1,),
        in_specs=[
            pl.BlockSpec(rest.shape, lambda _: (0, 0)),
            pl.BlockSpec(back[-1].shape, lambda _: (0, 0)),
            pl.BlockSpec(memory_space=pl.ANY),
        ],
        out_specs=pl.BlockSpec((kept, *result.shape[1:]), lambda _: (rows // kept - 1, 0, 0, 0)),
        out_shape=result,
        input_output_aliases={2: 0},
        compiler_params=pltpu.CompilerParams(vmem_limit_bytes=VMEM_LIMIT),
        name="sum_last",
    )(rest, back[-1], c)
    return c[None, None]


def solution(mesh):
    return jax.shard_map(
        functools.partial(local, dict(mesh.shape)),
        mesh=mesh,
        in_specs=(
            P("row", "col", "layer", None, None, None, None),
            P("row", "col", "layer", None, None),
            P("row", "col", "layer", None),
            P("row", "col", "layer", None, None, None, None),
            P("row", "col", "layer", None, None),
            P("row", "col", "layer", None),
            P("row", "col", None, None),
        ),
        out_specs=P("row", "col", "layer", None, None, None),
        check_vma=False,
    )
```

```python
import functools

import jax
import jax.numpy as jnp
from jax import lax
from jax.experimental import pallas as pl
from jax.experimental.pallas import tpu as pltpu
from jax.sharding import PartitionSpec as P

BS = 128
TOP = 32700.0
STEP = 0.08664339756999316
LEAST = 1e-33
TAIL = 16
SLOTS_A, SLOTS_C = 2, 2
B_COLS, B_COUNT, A_COLS, A_COUNT, C_COLS = 0, 2, 3, 5, 6
VMEM_LIMIT = 48 * 1024 * 1024


def row_product(a_ref, a_row, b_ref, r, a_lists, b_lists, c_lists):
    left, right = [], []
    for t in range(SLOTS_A):
        m = a_lists[A_COLS + t, r]
        live = t < a_lists[A_COUNT, r]
        wide = []
        for v in range(SLOTS_C):
            wanted = c_lists[C_COLS + v, r]
            slot = jnp.int32(0)
            found = jnp.int32(0)
            for u in range(b_ref.shape[1]):
                hit = live & (u < b_lists[B_COUNT, m]) & (b_lists[B_COLS + u, m] == wanted)
                slot = jnp.where(hit, jnp.int32(u), slot)
                found = jnp.where(hit, jnp.int32(1), found)
            block = b_ref[m, slot]
            wide.append(jnp.where(found == 1, block, jnp.zeros_like(block)))
        left.append(a_ref[pl.ds((a_row * SLOTS_A + t) * BS, BS), :])
        right.append(jnp.concatenate(wide, axis=1))
    return jnp.dot(
        jnp.concatenate(left, axis=1),
        jnp.concatenate(right, axis=0),
        preferred_element_type=jnp.float32,
    )


def pack_lists(b_cols, b_count, a_cols, a_count, c_cols):
    lists = [b_cols.T, b_count[None], a_cols.T, a_count[None], c_cols.T]
    depth, wide = sum(x.shape[0] for x in lists), b_count.shape[0]
    pack, at = 0, 0
    for x in lists:
        height = x.shape[0]
        pack += lax.pad(x, jnp.int32(0), [(at, depth - at - height, 0), (0, wide - x.shape[1], 0)])
        at += height
    return pack


def encode(value):
    peak = jnp.maximum(jnp.max(jnp.abs(value), axis=0, keepdims=True), LEAST)
    number = jnp.ceil(jnp.log(peak) * (1.0 / STEP))
    code = jnp.round(value * (TOP * jnp.exp(number * -STEP)))
    code = jnp.clip(code, -32767.0, 32767.0)
    return code.astype(jnp.int32).astype(jnp.int16), number.astype(jnp.int32)


def decode(code, number):
    scale = jnp.exp(number.astype(jnp.float32) * STEP) * (1.0 / TOP)
    return code.astype(jnp.int32).astype(jnp.float32) * scale


def store_payload(out_ref, products):
    numbers = []
    for k, value in enumerate(products):
        code, number = encode(value)
        for v in range(SLOTS_C):
            out_ref[pl.ds((k * SLOTS_C + v) * BS, BS), :] = code[:, v * BS : (v + 1) * BS]
            numbers.append(number[:, v * BS : (v + 1) * BS])
    size = len(numbers) * BS
    numbers += [jnp.zeros_like(numbers[0])] * (TAIL - len(numbers))
    out_ref[pl.ds(size, TAIL), :] = jnp.concatenate(numbers, axis=0).astype(jnp.int16)


def head_kernel(first, pack_ref, a_hbm, out_ref, tile, sem):
    size = out_ref.shape[0] - TAIL
    start = pl.multiple_of(first[0] * SLOTS_A * BS, BS)
    copy = pltpu.make_async_copy(a_hbm.at[pl.ds(start, size)], out_ref.at[pl.ds(0, size)], sem)
    copy.start()
    tile[...] = jnp.zeros_like(tile)
    tile[pl.ds(0, pack_ref.shape[0]), pl.ds(0, pack_ref.shape[1])] = pack_ref[...].astype(jnp.float32)
    out_ref[pl.ds(size, TAIL), :] = tile[...].astype(out_ref.dtype)
    copy.wait()


def local_kernel(parts, half, pack, a_ref, b_ref, own_ref, out_ref, *sent):
    rows = a_ref.shape[0] // (2 * SLOTS_A * BS)
    other = (1 - half[0]) * rows
    own = half[0] * rows
    for (same, start, _), ref in zip(parts, sent, strict=True):
        at = pl.multiple_of((jnp.where(same, own, other) + start) * SLOTS_A * BS, BS)
        ref[...] = a_ref[pl.ds(at, ref.shape[0]), :]
    store_payload(
        out_ref, [row_product(a_ref, other + k, b_ref, other + k, pack, pack, pack) for k in range(rows)]
    )
    for k in range(rows):
        own_ref[pl.ds(k * BS, BS), :] = row_product(a_ref, own + k, b_ref, own + k, pack, pack, pack)


def remote_kernel(first, a_lists, b_lists, c_lists, a_ref, b_ref, out_ref):
    rows = a_ref.shape[0] // (SLOTS_A * BS)
    store_payload(
        out_ref,
        [row_product(a_ref, k, b_ref, first[0] + k, a_lists, b_lists, c_lists) for k in range(rows)],
    )


def payload_row(ref, k):
    tail = ref[pl.ds(ref.shape[0] - TAIL, TAIL), :].astype(jnp.int32)
    blocks = range(k * SLOTS_C, (k + 1) * SLOTS_C)
    return jnp.concatenate([decode(ref[pl.ds(n * BS, BS), :], tail[n : n + 1, :]) for n in blocks], axis=1)


def add_kernel(part, half, total_ref, part_ref, *refs):
    *layer, out_ref = refs
    _, start, count = part
    for k in range(count):
        at = pl.ds((start + k) * BS, BS)
        out_ref[at, :] = total_ref[at, :] + payload_row(part_ref, k)
    for layer_ref in layer:

        @pl.when(half[0] == 0)
        def _():
            for k in range(out_ref.shape[0] // BS):
                out_ref[pl.ds(k * BS, BS), :] += payload_row(layer_ref, k)


def store_row(out_ref, k, total):
    for v in range(SLOTS_C):
        out_ref[k, v] = total[:, v * BS : (v + 1) * BS].astype(out_ref.dtype)


def early_sum_kernel(part, kept, half, total_ref, layer_ref, part_ref, out_ref, rest_ref):
    rows = out_ref.shape[0]
    _, start, count = part
    for k in range(rows):
        total = total_ref[pl.ds(k * BS, BS), :]
        if start <= k < start + count:
            total = total + payload_row(part_ref, k - start)
        total = total + jnp.where(half[0] == 1, payload_row(layer_ref, k), 0.0)
        if k < rows - kept:
            store_row(out_ref, k, total)
        else:
            rest_ref[pl.ds((k - rows + kept) * BS, BS), :] = total


def last_sum_kernel(rest_ref, part_ref, _, out_ref):
    for k in range(out_ref.shape[0]):
        store_row(out_ref, k, rest_ref[pl.ds(k * BS, BS), :] + payload_row(part_ref, k))


SMEM = pl.BlockSpec(memory_space=pltpu.SMEM)
VMEM = pl.BlockSpec(memory_space=pltpu.VMEM)
HBM = pl.BlockSpec(memory_space=pltpu.HBM)


def call(kernel, scalars, arrays, outs, cost, name, out_specs=None, **more):
    return pl.pallas_call(
        kernel,
        in_specs=[SMEM] * len(scalars) + [VMEM] * len(arrays),
        out_specs=jax.tree.map(lambda _: VMEM, outs) if out_specs is None else out_specs,
        out_shape=outs,
        compiler_params=pltpu.CompilerParams(vmem_limit_bytes=VMEM_LIMIT),
        cost_estimate=pl.CostEstimate(flops=int(cost * US), bytes_accessed=0, transcendentals=0),
        name=name,
        **more,
    )(*scalars, *arrays)


PARTS = ((False, 0, 4), (False, 4, 4), (True, 0, 4), (True, 4, 4))
US = 1e9
COST_STEP0 = 2
COST_STEP1 = 25
COST_FIRST = 6
COST_SUM = 1


def after(value, *others):
    return lax.optimization_barrier((value, *others))[0]


def local(mesh_shape, a_blocks, a_cols, a_count, b_blocks, b_cols, b_count, c_cols):
    n_row, n_col = mesh_shape["row"], mesh_shape["col"]
    a_panel, b_panel = a_blocks[0, 0, 0], b_blocks[0, 0, 0]
    a_index, a_live = a_cols[0, 0, 0], a_count[0, 0, 0]
    b_index, b_live = b_cols[0, 0, 0], b_count[0, 0, 0]
    out_cols = c_cols[0, 0]
    layer = lax.axis_index("layer").astype(jnp.int32)
    rows = a_panel.shape[0] // 2
    wide = out_cols.shape[1] * BS
    summed = jax.ShapeDtypeStruct((rows * BS, wide), jnp.float32)
    result = jax.ShapeDtypeStruct((rows, out_cols.shape[1], BS, BS), jnp.bfloat16)

    def coded(count):
        return jax.ShapeDtypeStruct((count * SLOTS_C * BS + TAIL, BS), jnp.int16)

    def place(i, j, l):
        return ((i % n_row) * n_col + j % n_col) * 2 + l

    grid = [(i, j, l) for i in range(n_row) for j in range(n_col) for l in range(2)]

    def send(name, value, target, who=(0, 1)):
        pairs = [(place(i, j, l), place(*target(i, j, l))) for i, j, l in grid if l in who]
        with jax.named_scope(name):
            return lax.ppermute(value, ("row", "col", "layer"), pairs)

    def to_user(i, j, l):
        return i + 1, j - 1, l

    half = layer[None]
    firsts = [jnp.where(same, layer, 1 - layer) * rows + start for same, start, _ in PARTS]

    pack = pack_lists(b_index, b_live, a_index, a_live, out_cols)
    row_size = SLOTS_A * BS
    a_panel = a_panel.reshape(-1, BS)
    head = pl.pallas_call(
        head_kernel,
        in_specs=[SMEM, VMEM, HBM],
        out_specs=VMEM,
        out_shape=jax.ShapeDtypeStruct((PARTS[0][2] * row_size + TAIL, BS), a_panel.dtype),
        scratch_shapes=[pltpu.VMEM((TAIL, BS), jnp.float32), pltpu.SemaphoreType.DMA],
        compiler_params=pltpu.CompilerParams(vmem_limit_bytes=VMEM_LIMIT),
        name="head",
    )(firsts[0][None], pack, a_panel)
    far_a = [send("send_a0", head, to_user)]

    parts = PARTS[1:]
    own, other, *a_parts = call(
        functools.partial(local_kernel, parts),
        (half, pack),
        (a_panel, b_panel),
        (
            summed,
            coded(rows),
            *(jax.ShapeDtypeStruct((count * row_size, BS), a_panel.dtype) for _, _, count in parts),
        ),
        COST_STEP0,
        "step0",
    )
    down = send("send_layer_down", other, lambda i, j, l: (i, j, 0), who=(1,))
    far_cols = send("send_c_cols", after(pack, other), lambda i, j, l: (i + 1, j, l))
    far_a.append(send("send_a1", a_parts[0], to_user))

    far_lists = far_a[0][-TAIL:, : pack.shape[1]].astype(jnp.int32)
    back, before = [], []
    for k, ((same, _, count), first) in enumerate(zip(PARTS, firsts, strict=True)):
        product = call(
            remote_kernel,
            (first[None], far_lists, pack, far_cols),
            (after(far_a[k], *before), b_panel),
            coded(count),
            COST_FIRST if k == 0 else COST_STEP1,
            f"step1_part{k}",
        )
        before = [product]
        if k == 0:
            before.append(down)
        if k + 1 < len(a_parts):
            far_a.append(send(f"send_a{k + 2}", after(a_parts[k + 1], product), to_user))
        if k == len(PARTS) - 3:
            up = send("send_layer_up", after(other, product), lambda i, j, l: (i, j, 1), who=(0,))
        back.append(send(f"send_c{k}", product, lambda i, j, l, same=same: (i - 1, j, l if same else 1 - l)))
    total, more = own, (down,)
    for k, part in enumerate(PARTS[:-2]):
        total = call(
            functools.partial(add_kernel, part),
            (half,),
            (total, back[k], *more),
            summed,
            COST_SUM,
            f"sum_part{k}",
            input_output_aliases={1: 0},
        )
        more = ()
    kept = PARTS[-1][2]
    rest = jax.ShapeDtypeStruct((kept * BS, wide), jnp.float32)
    c, rest = call(
        functools.partial(early_sum_kernel, PARTS[-2], kept), (half,), (total, up, back[-2]), (result, rest), COST_SUM, "sum_early"
    )
    c = pl.pallas_call(
        last_sum_kernel,
        grid=(1,),
        in_specs=[
            pl.BlockSpec(rest.shape, lambda _: (0, 0)),
            pl.BlockSpec(back[-1].shape, lambda _: (0, 0)),
            pl.BlockSpec(memory_space=pl.ANY),
        ],
        out_specs=pl.BlockSpec((kept, *result.shape[1:]), lambda _: (rows // kept - 1, 0, 0, 0)),
        out_shape=result,
        input_output_aliases={2: 0},
        compiler_params=pltpu.CompilerParams(vmem_limit_bytes=VMEM_LIMIT),
        name="sum_last",
    )(rest, back[-1], c)
    return c[None, None]


def solution(mesh):
    return jax.shard_map(
        functools.partial(local, dict(mesh.shape)),
        mesh=mesh,
        in_specs=(
            P("row", "col", "layer", None, None, None, None),
            P("row", "col", "layer", None, None),
            P("row", "col", "layer", None),
            P("row", "col", "layer", None, None, None, None),
            P("row", "col", "layer", None, None),
            P("row", "col", "layer", None),
            P("row", "col", None, None),
        ),
        out_specs=P("row", "col", "layer", None, None, None),
        check_vma=False,
    )
```
